256 devices in a mesh: ctx: 64 (over x, y, z_hi, core), chan: 4 (over z_lo).
Axes of the slice: x: 4, y: 4, z: 8 (z_hi: 2, z_lo: 4; z = z_hi * 4 + z_lo), core: 2. Of those that a mesh axis runs over, the one named last changes fastest.
Arguments:
- query_proj: bfloat16 [24576, 4096], P('ctx', 'chan'), may hold values from -6 to 6
- key_proj: bfloat16 [24576, 4096], P('ctx', 'chan'), may hold values from -6 to 6
- value_proj: bfloat16 [24576, 4096], P('ctx', 'chan'), may hold values from -6 to 6
- filter_taps: float32 [24576, 4096], P('ctx', 'chan'), may hold values from -1.1 to 1.1
- skip_gain: float32 [4096], P('chan'), may hold values from -4 to 4
- out_weight: bfloat16 [4096, 4096], P('chan'), may hold values from -0.09375 to 0.09375
Outputs:
- mixed_out: bfloat16 [24576, 4096], P('ctx', 'chan')
The draws below stay inside these ranges and needn't reach their ends.
All inputs are finite; a program needn't handle non-finite values.
Results may differ from the reference program's by a relative error of at most 0.0049.
Values may be sent and summed in bfloat16 or wider, within the bound.
A program may use at most 128 MiB of HBM per device.

```python
import jax
import jax.numpy as jnp
from jax import lax

CHANNELS = 4096
DOUT = 4096
LENGTH = 24576


def draw_filter_taps(key, part):
    key = jax.random.fold_in(key, 11)
    rate_key, tap_key = jax.random.split(key)
    low_log = jnp.log(30.0)
    high_log = jnp.log(3.0 * LENGTH)
    spans = jnp.exp(jax.random.uniform(rate_key, (1, CHANNELS), jnp.float32, low_log, high_log))
    lags = jnp.arange(LENGTH, dtype=jnp.float32)[:, None]
    ratio = jnp.exp(-2.0 / spans)
    scaling = jnp.sqrt((1.0 - ratio) / (1.0 - ratio ** LENGTH))
    taps = jax.random.truncated_normal(tap_key, -4.0, 4.0, (LENGTH, CHANNELS), jnp.float32)
    return taps * jnp.exp(-lags / spans) * scaling


def block_scale(own_key, shape, pieces, low, top_value):
    level = 1.0
    for dim, shards_of in pieces:
        draws = jax.random.uniform(jax.random.fold_in(jax.random.fold_in(own_key, 6), dim), (shards_of,), jnp.float32, low / len(pieces), top_value / len(pieces))
        level = level * jnp.repeat(jnp.exp(draws), shape[dim] // shards_of).reshape((-1,) + (1,) * (len(shape) - 1 - dim))
    return level


def gaussian(stream_key, extent, width, bound, shards=(), kind=jnp.bfloat16):
    entries = width * jax.random.normal(stream_key, extent, jnp.float32)
    if shards:
        entries = entries * block_scale(stream_key, extent, shards, -0.22, 0.18)
    return jnp.clip(entries, -bound, bound).astype(kind)


def setup_inputs(seed: int = 0) -> dict:
    splits = jax.random.split(jax.random.key(seed), 7)
    query_proj = gaussian(splits[0], (LENGTH, CHANNELS), 1.0, 6.0, ((0, 64), (1, 4)))
    key_proj = gaussian(splits[1], (LENGTH, CHANNELS), 1.0, 6.0, ((0, 64), (1, 4)))
    value_proj = gaussian(splits[2], (LENGTH, CHANNELS), 1.0, 6.0, ((0, 64), (1, 4)))
    filter_taps = draw_filter_taps(jax.random.fold_in(splits[6], 71), 0)
    skip_gain = gaussian(splits[4], (CHANNELS,), 1.0, 4.0, ((0, 4),), jnp.float32)
    out_weight = gaussian(splits[5], (CHANNELS, DOUT), CHANNELS ** -0.5, 0.09375, ((0, 4),))
    return {"query_proj": query_proj, "key_proj": key_proj, "value_proj": value_proj, "filter_taps": filter_taps, "skip_gain": skip_gain, "out_weight": out_weight}


def block_conv(operands):
    signal_block, filter_block = operands
    padded = 2 * LENGTH
    product = jnp.fft.rfft(signal_block, n=padded, axis=0) * jnp.fft.rfft(filter_block, n=padded, axis=0)
    return jnp.fft.irfft(product, n=padded, axis=0)[:LENGTH]


def reference(query_proj, key_proj, value_proj, filter_taps, skip_gain, out_weight):
    signal = key_proj.astype(jnp.float32) * value_proj.astype(jnp.float32)
    block_total = CHANNELS // 64
    signal_blocks = signal.reshape(LENGTH, block_total, 64).transpose(1, 0, 2)
    filter_blocks = filter_taps.reshape(LENGTH, block_total, 64).transpose(1, 0, 2)
    conv_blocks = lax.map(block_conv, (signal_blocks, filter_blocks))
    conv = conv_blocks.transpose(1, 0, 2).reshape(LENGTH, CHANNELS).astype(signal.dtype)
    gated = (query_proj.astype(jnp.float32) * (conv + skip_gain[None, :] * signal)).astype(jnp.bfloat16)
    return jnp.dot(gated, out_weight, preferred_element_type=jnp.float32).astype(jnp.bfloat16)
```

```python
import functools
import math

import jax
import jax.numpy as jnp
import numpy as np
import ml_dtypes
from jax import lax
from jax.experimental import pallas as pl
from jax.experimental.pallas import tpu as pltpu
from jax.sharding import PartitionSpec as P

BF16 = jnp.bfloat16
F32 = jnp.float32
LANE = 128


def split_const(table):
    high = table.astype(np.float32).astype(ml_dtypes.bfloat16)
    low = (table - high.astype(np.float64)).astype(np.float32).astype(ml_dtypes.bfloat16)
    return high, low


def dft_tables(blocks, tok_rows):
    sub = tok_rows // LANE
    half = blocks * sub
    outer = 2 * half
    full = outer * LANE
    order = (np.arange(blocks)[None, :] * sub + np.arange(sub)[:, None]).reshape(-1)
    freq = np.arange(half) + 0.5
    phase = 2.0 * math.pi * ((order[None, :] * (2 * np.arange(half)[:, None] + 1)) % (2 * outer)) / (2 * outer)
    first = np.concatenate([np.cos(phase), -np.sin(phase)], 0)
    back = np.concatenate([np.cos(phase).T, -np.sin(phase).T], 1) * (2.0 / full)
    turn = 2.0 * math.pi * np.arange(LANE)[None, :] * freq[:, None] / full
    inner = 2.0 * math.pi * ((np.arange(LANE)[:, None] * np.arange(LANE)[None, :]) % LANE) / LANE
    c, s = np.cos(inner), np.sin(inner)
    forward = np.block([[c, -s], [s, c]])
    inverse = np.block([[c, s], [-s, c]])
    return (
        *split_const(first),
        *split_const(forward),
        *split_const(inverse),
        *split_const(back),
        np.cos(turn).astype(np.float32),
        np.sin(turn).astype(np.float32),
    )


def dot(a, b):
    return jnp.dot(a, b, preferred_element_type=F32)


def split(x):
    high = x.astype(BF16)
    low = (x - high.astype(F32)).astype(BF16)
    return high, low


def dot3(x, m_hi, m_lo):
    hi, lo = split(x)
    return dot(hi, m_hi) + dot(lo, m_hi) + dot(hi, m_lo)


def prep_kernel(k_ref, v_ref, f_ref, s_out, f_out):
    s = k_ref[...].astype(F32) * v_ref[...].astype(F32)
    s_out[...] = s.T.astype(BF16)
    f_out[...] = f_ref[...].T.astype(BF16)


def prep(k, v, f):
    rows, width = k.shape
    step = 256
    spec = pl.BlockSpec((rows, step), lambda i: (0, i))
    out = pl.BlockSpec((step, rows), lambda i: (i, 0))
    shape = jax.ShapeDtypeStruct((width, rows), BF16)
    return pl.pallas_call(
        prep_kernel,
        grid=(width // step,),
        in_specs=[spec] * 3,
        out_specs=[out, out],
        out_shape=[shape, shape],
    )(k, v, f)


def conv_kernel(
    blocks, group, sub,
    s_ref, f_ref, a_hi, a_lo, fw_hi, fw_lo, iv_hi, iv_lo, bk_hi, bk_lo, cos_ref, sin_ref,
    out_ref, s_wide, f_wide, o_wide,
):
    half = blocks * sub
    for a in range(sub):
        s_wide[a] = s_ref[:, a * LANE:(a + 1) * LANE].astype(F32)
        f_wide[a] = f_ref[:, a * LANE:(a + 1) * LANE].astype(F32)

    def columns(wide, c):
        parts = [
            wide.at[a][pl.ds(c, blocks, stride=group), :] for a in range(sub)
        ]
        return jnp.concatenate(parts, 0).astype(BF16)

    def step(p, _):
        chans = (2 * p, 2 * p + 1)
        x = jnp.concatenate(
            [columns(s_wide, c) for c in chans] + [columns(f_wide, c) for c in chans], 1
        )
        y = dot(a_hi[...], x) + dot(a_lo[...], x)
        cos, sin = cos_ref[...], sin_ref[...]
        spectra = []
        for j in range(4):
            re = y[:half, j * LANE:(j + 1) * LANE]
            im = y[half:, j * LANE:(j + 1) * LANE]
            turned = jnp.concatenate([re * cos + im * sin, im * cos - re * sin], 1)
            spectra.append(dot3(turned, fw_hi[...], fw_lo[...]))
        backs = []
        for j in range(2):
            s, f = spectra[j], spectra[2 + j]
            s_re, s_im, f_re, f_im = s[:, :LANE], s[:, LANE:], f[:, :LANE], f[:, LANE:]
            product = jnp.concatenate([s_re * f_re - s_im * f_im, s_re * f_im + s_im * f_re], 1)
            g = dot3(product, iv_hi[...], iv_lo[...])
            re, im = g[:, :LANE], g[:, LANE:]
            backs.append(jnp.concatenate([re * cos - im * sin, im * cos + re * sin], 0))
        z_hi, z_lo = split(jnp.concatenate(backs, 1))
        res = dot(bk_hi[...], z_hi) + dot(bk_hi[...], z_lo) + dot(bk_lo[...], z_hi)
        for j, c in enumerate(chans):
            for a in range(sub):
                o_wide.at[a][pl.ds(c, blocks, stride=group), :] = res[
                    a * blocks:(a + 1) * blocks, j * LANE:(j + 1) * LANE
                ]
        return 0

    lax.fori_loop(0, group // 2, step, 0)
    for a in range(sub):
        out_ref[:, a * LANE:(a + 1) * LANE] = o_wide[a].astype(BF16)


def long_conv(s, f, blocks):
    total, rows = s.shape
    group = total // blocks
    sub = rows // LANE
    tables = dft_tables(blocks, rows)
    wide = pltpu.VMEM((sub, total, LANE), F32)
    return pl.pallas_call(
        functools.partial(conv_kernel, blocks, group, sub),
        out_shape=jax.ShapeDtypeStruct((total, rows), BF16),
        scratch_shapes=[wide, wide, wide],
        compiler_params=pltpu.CompilerParams(vmem_limit_bytes=48 * 1024 * 1024),
    )(s, f, *[jnp.asarray(t) for t in tables])


def gate_kernel(c_ref, q_ref, k_ref, v_ref, g_ref, out_ref):
    signal = k_ref[...].astype(F32) * v_ref[...].astype(F32)
    conv = c_ref[...].astype(F32).T
    out_ref[...] = (q_ref[...].astype(F32) * (conv + g_ref[...] * signal)).astype(BF16)


def gate(conv, q, k, v, gain):
    rows, width = q.shape
    step = 256
    spec = pl.BlockSpec((rows, step), lambda i: (0, i))
    return pl.pallas_call(
        gate_kernel,
        grid=(width // step,),
        in_specs=[
            pl.BlockSpec((step, rows), lambda i: (i, 0)),
            spec, spec, spec,
            pl.BlockSpec((1, step), lambda i: (0, i)),
        ],
        out_specs=spec,
        out_shape=jax.ShapeDtypeStruct((rows, width), BF16),
    )(conv, q, k, v, gain)


def per_device(query_proj, key_proj, value_proj, filter_taps, skip_gain, out_weight):
    blocks = lax.axis_size("ctx")
    s, f = prep(key_proj, value_proj, filter_taps)
    s = lax.all_to_all(s, "ctx", split_axis=0, concat_axis=0, tiled=True)
    f = lax.all_to_all(f, "ctx", split_axis=0, concat_axis=0, tiled=True)
    conv = long_conv(s, f, blocks)
    conv = lax.all_to_all(conv, "ctx", split_axis=0, concat_axis=0, tiled=True)
    gated = gate(conv, query_proj, key_proj, value_proj, skip_gain[None, :])
    partial_sums = jnp.dot(gated, out_weight, preferred_element_type=F32).astype(BF16)
    return lax.psum_scatter(partial_sums, "chan", scatter_dimension=1, tiled=True)


def solution(mesh):
    placed = (
        P("ctx", "chan"),
        P("ctx", "chan"),
        P("ctx", "chan"),
        P("ctx", "chan"),
        P("chan"),
        P("chan", None),
    )
    return jax.shard_map(
        per_device, mesh=mesh, in_specs=placed, out_specs=P("ctx", "chan"), check_vma=False
    )
```

```python
import functools
import math

import jax
import jax.numpy as jnp
import numpy as np
import ml_dtypes
from jax import lax
from jax.experimental import pallas as pl
from jax.experimental.pallas import tpu as pltpu
from jax.sharding import PartitionSpec as P

BF16 = jnp.bfloat16
F32 = jnp.float32
LANE = 128


def split_const(table):
    high = table.astype(np.float32).astype(ml_dtypes.bfloat16)
    low = (table - high.astype(np.float64)).astype(np.float32).astype(ml_dtypes.bfloat16)
    return high, low


def dft_tables(blocks, tok_rows):
    sub = tok_rows // LANE
    half = blocks * sub
    outer = 2 * half
    full = outer * LANE
    order = (np.arange(blocks)[None, :] * sub + np.arange(sub)[:, None]).reshape(-1)
    freq = np.arange(half) + 0.5
    phase = 2.0 * math.pi * ((order[None, :] * (2 * np.arange(half)[:, None] + 1)) % (2 * outer)) / (2 * outer)
    first = np.concatenate([np.cos(phase), -np.sin(phase)], 0)
    back = np.concatenate([np.cos(phase).T, -np.sin(phase).T], 1) * (2.0 / full)
    turn = 2.0 * math.pi * np.arange(LANE)[None, :] * freq[:, None] / full
    inner = 2.0 * math.pi * ((np.arange(LANE)[:, None] * np.arange(LANE)[None, :]) % LANE) / LANE
    c, s = np.cos(inner), np.sin(inner)
    forward = np.block([[c, -s], [s, c]])
    inverse = np.block([[c, s], [-s, c]])
    return (
        *split_const(first),
        *split_const(forward),
        *split_const(inverse),
        *split_const(back),
        np.cos(turn).astype(np.float32),
        np.sin(turn).astype(np.float32),
    )


def dot(a, b):
    return jnp.dot(a, b, preferred_element_type=F32)


def split(x):
    high = x.astype(BF16)
    low = (x - high.astype(F32)).astype(BF16)
    return high, low


def dot3(x, m_hi, m_lo):
    hi, lo = split(x)
    return dot(hi, m_hi) + dot(lo, m_hi) + dot(hi, m_lo)


MESH = pl.DeviceIdType.MESH
COLS = 256


def whole_kernel(
    blocks, group, sub, width,
    q_hbm, k_hbm, v_hbm, f_hbm, gain_hbm, w_hbm,
    first_hi, first_lo, fw_hi_in, fw_lo_in, iv_hi_in, iv_lo_in, bk_hi_in, bk_lo_in, cos_in, sin_in,
    out_hbm,
    q_v, k_v, v_v, f_v, gain_v, w_own, w_near,
    a_hi, a_lo, fw_hi, fw_lo, iv_hi, iv_lo, bk_hi, bk_lo, cos_ref, sin_ref,
    send_f, send_s, send_c, recv_f, recv_s, recv_c,
    wide_a, wide_b, spec_f,
    g_own, g_near, part_out, part_in, part_own, out_v,
    load_sem, table_sem, own_sem, store_sem,
    a2a_send, a2a_recv, wz_send, wz_recv, wx_send, wx_recv, wc_send, wc_recv,
    g_send, g_recv, p_send, p_recv,
):
    c = lax.axis_index("ctx")
    h = lax.axis_index("chan")
    near = h + 1 - 2 * lax.rem(h, 2)
    far = lax.rem(h + 2, 4)
    far_near = lax.rem(near + 2, 4)
    core = lax.rem(c, 2)
    sibling = c + 1 - 2 * core
    plane = lax.rem(c, 4)
    spot = lax.div(c, 4)
    spots = blocks // 4
    rows = sub * LANE
    half = blocks * sub
    slab = width // blocks * 2

    bar = pltpu.get_barrier_semaphore()

    def greet(j, _):
        pl.semaphore_signal(
            bar, inc=1, device_id=(lax.rem(c + j, blocks), h), device_id_type=MESH
        )
        return 0

    loads = [
        pltpu.make_async_copy(src, dst, load_sem.at[i])
        for i, (src, dst) in enumerate(
            [
                (f_hbm, f_v),
                (k_hbm, k_v),
                (v_hbm, v_v),
                (q_hbm, q_v),
                (gain_hbm, gain_v),
                (w_hbm.at[:, pl.ds(pl.multiple_of(h * width, width), width)], w_own.at[:, pl.ds(0, width)]),
                (w_hbm.at[:, pl.ds(pl.multiple_of(far * width, width), width)], w_own.at[:, pl.ds(width, width)]),
            ]
        )
    ]
    tables = [
        pltpu.make_async_copy(src, dst, table_sem.at[i])
        for i, (src, dst) in enumerate(
            zip(
                (first_hi, first_lo, fw_hi_in, fw_lo_in, iv_hi_in, iv_lo_in, bk_hi_in, bk_lo_in, cos_in, sin_in),
                (a_hi, a_lo, fw_hi, fw_lo, iv_hi, iv_lo, bk_hi, bk_lo, cos_ref, sin_ref),
            )
        )
    ]
    for copy in loads[:3]:
        copy.start()
    lax.fori_loop(1, blocks, greet, 0)
    for other in (near, far):
        pl.semaphore_signal(bar, inc=1, device_id=(c, other), device_id_type=MESH)
    for copy in loads[3:] + tables:
        copy.start()

    def a2a_copy(i, src, dst, j):
        to = lax.rem(c + j, blocks)
        return pltpu.make_async_remote_copy(
            src_ref=src.at[pl.ds(pl.multiple_of(to * group, group), group)],
            dst_ref=dst.at[pl.ds(pl.multiple_of(c * group, group), group)],
            send_sem=a2a_send.at[i],
            recv_sem=a2a_recv.at[i],
            device_id=(to, h),
            device_id_type=MESH,
        )

    def own_copy(i, src, dst):
        mine = pl.ds(pl.multiple_of(c * group, group), group)
        return pltpu.make_async_copy(src.at[mine], dst.at[mine], own_sem.at[i])

    def a2a_start(i, src, dst):
        def send(j, _):
            a2a_copy(i, src, dst, j).start()
            return 0

        own_copy(i, src, dst).start()
        lax.fori_loop(1, blocks, send, 0)

    def a2a_all(i, src, dst):
        most = pl.ds(0, (blocks - 1) * group)
        return pltpu.make_async_remote_copy(
            src_ref=src.at[most],
            dst_ref=dst.at[most],
            send_sem=a2a_send.at[i],
            recv_sem=a2a_recv.at[i],
            device_id=(sibling, h),
            device_id_type=MESH,
        )

    def a2a_arrived(i, src, dst):
        own_copy(i, src, dst).wait()
        a2a_all(i, src, dst).wait_recv()

    loads[0].wait()
    for i in range(width // COLS):
        send_f[i * COLS:(i + 1) * COLS, :] = f_v[:, i * COLS:(i + 1) * COLS].T.astype(BF16)
    pl.semaphore_wait(bar, blocks + 1)

    my_rows = pl.ds(pl.multiple_of(core * (width // 2) + spot * slab, slab), slab)

    def near_slice(i, block):
        return pltpu.make_async_remote_copy(
            src_ref=w_hbm.at[my_rows, pl.ds(pl.multiple_of(block * width, width), width)],
            dst_ref=w_near.at[my_rows, pl.ds(i * width, width)],
            send_sem=wz_send.at[i],
            recv_sem=wz_recv.at[i],
            device_id=(c, near),
            device_id_type=MESH,
        )

    near_copies = [near_slice(0, near), near_slice(1, far_near)]
    for copy in near_copies:
        copy.start()
    a2a_start(0, send_f, recv_f)

    loads[1].wait()
    loads[2].wait()
    for i in range(width // COLS):
        piece = slice(i * COLS, (i + 1) * COLS)
        signal = k_v[:, piece].astype(F32) * v_v[:, piece].astype(F32)
        send_s[piece, :] = signal.T.astype(BF16)
    a2a_start(1, send_s, recv_s)

    for copy in near_copies:
        copy.wait_recv()

    def spread(j, _):
        to = lax.rem(spot + j, spots) * 4 + plane
        pltpu.make_async_remote_copy(
            src_ref=w_near.at[my_rows],
            dst_ref=w_near.at[my_rows],
            send_sem=wx_send,
            recv_sem=wx_recv,
            device_id=(to, h),
            device_id_type=MESH,
        ).start()
        return 0

    lax.fori_loop(1, spots, spread, 0)
    spread_rows = pl.ds(0, (spots - 1) * slab)
    spread_all = pltpu.make_async_remote_copy(
        src_ref=w_near.at[spread_rows],
        dst_ref=w_near.at[spread_rows],
        send_sem=wx_send,
        recv_sem=wx_recv,
        device_id=(sibling, h),
        device_id_type=MESH,
    )
    core_rows = pl.ds(pl.multiple_of(core * (width // 2), width // 2), width // 2)
    to_sibling = pltpu.make_async_remote_copy(
        src_ref=w_near.at[core_rows],
        dst_ref=w_near.at[core_rows],
        send_sem=wc_send,
        recv_sem=wc_recv,
        device_id=(sibling, h),
        device_id_type=MESH,
    )

    for copy in tables:
        copy.wait()

    def widen(src, wide):
        for a in range(sub):
            wide[a] = src[:, a * LANE:(a + 1) * LANE].astype(F32)

    def columns(wide, ch):
        parts = [wide.at[a][pl.ds(ch, blocks, stride=group), :] for a in range(sub)]
        return jnp.concatenate(parts, 0).astype(BF16)

    def spectra(wide, chans):
        x = jnp.concatenate([columns(wide, ch) for ch in chans], 1)
        y = dot(a_hi[...], x) + dot(a_lo[...], x)
        cos, sin = cos_ref[...], sin_ref[...]
        found = []
        for j in range(len(chans)):
            re = y[:half, j * LANE:(j + 1) * LANE]
            im = y[half:, j * LANE:(j + 1) * LANE]
            turned = jnp.concatenate([re * cos + im * sin, im * cos - re * sin], 1)
            found.append(dot3(turned, fw_hi[...], fw_lo[...]))
        return found

    a2a_arrived(0, send_f, recv_f)
    widen(recv_f, wide_a)

    def taps_step(p, _):
        chans = (2 * p, 2 * p + 1)
        for ch, spec in zip(chans, spectra(wide_a, chans)):
            spec_f[ch] = spec
        return 0

    lax.fori_loop(0, group // 2, taps_step, 0)

    a2a_arrived(1, send_s, recv_s)
    widen(recv_s, wide_a)

    def conv_step(p, _):
        chans = (2 * p, 2 * p + 1)
        cos, sin = cos_ref[...], sin_ref[...]
        backs = []
        for ch, s in zip(chans, spectra(wide_a, chans)):
            f = spec_f[ch]
            s_re, s_im, f_re, f_im = s[:, :LANE], s[:, LANE:], f[:, :LANE], f[:, LANE:]
            product = jnp.concatenate([s_re * f_re - s_im * f_im, s_re * f_im + s_im * f_re], 1)
            g = dot3(product, iv_hi[...], iv_lo[...])
            re, im = g[:, :LANE], g[:, LANE:]
            backs.append(jnp.concatenate([re * cos - im * sin, im * cos + re * sin], 0))
        z_hi, z_lo = split(jnp.concatenate(backs, 1))
        res = dot(bk_hi[...], z_hi) + dot(bk_hi[...], z_lo) + dot(bk_lo[...], z_hi)
        for j, ch in enumerate(chans):
            for a in range(sub):
                wide_b.at[a][pl.ds(ch, blocks, stride=group), :] = res[
                    a * blocks:(a + 1) * blocks, j * LANE:(j + 1) * LANE
                ]
        return 0

    lax.fori_loop(0, group // 2, conv_step, 0)
    for a in range(sub):
        send_c[:, a * LANE:(a + 1) * LANE] = wide_b[a].astype(BF16)
    a2a_start(2, send_c, recv_c)

    spread_all.wait_recv()
    to_sibling.start()
    for copy in loads[3:]:
        copy.wait()
    a2a_arrived(2, send_c, recv_c)

    swaps = []
    for t in range(sub):
        here = slice(t * LANE, (t + 1) * LANE)
        for i in range(width // COLS):
            piece = slice(i * COLS, (i + 1) * COLS)
            conv = recv_c[piece, here].astype(F32).T
            signal = k_v[here, piece].astype(F32) * v_v[here, piece].astype(F32)
            g_own[t, :, piece] = (
                q_v[here, piece].astype(F32) * (conv + gain_v[:, piece] * signal)
            ).astype(BF16)
        swap = pltpu.make_async_remote_copy(
            src_ref=g_own.at[t],
            dst_ref=g_near.at[t],
            send_sem=g_send.at[t],
            recv_sem=g_recv.at[t],
            device_id=(c, near),
            device_id_type=MESH,
        )
        swap.start()
        swaps.append(swap)

    to_sibling.wait_recv()
    parts = []
    for t in range(sub):
        swaps[t].wait_recv()

        def project(i, _, t=t):
            cols = pl.ds(pl.multiple_of(width + i * COLS, COLS), COLS)
            part_out[t, :, pl.ds(pl.multiple_of(i * COLS, COLS), COLS)] = (
                dot(g_own[t], w_own[:, cols]) + dot(g_near[t], w_near[:, cols])
            ).astype(BF16)
            return 0

        lax.fori_loop(0, width // COLS, project, 0)
        part = pltpu.make_async_remote_copy(
            src_ref=part_out.at[t],
            dst_ref=part_in.at[t],
            send_sem=p_send.at[t],
            recv_sem=p_recv.at[t],
            device_id=(c, far),
            device_id_type=MESH,
        )
        part.start()
        parts.append(part)
    for t in range(sub):

        def project_own(i, _, t=t):
            cols = pl.ds(pl.multiple_of(i * COLS, COLS), COLS)
            part_own[t, :, cols] = dot(g_own[t], w_own[:, cols]) + dot(g_near[t], w_near[:, cols])
            return 0

        lax.fori_loop(0, width // COLS, project_own, 0)
    stores = []
    for t in range(sub):
        parts[t].wait_recv()
        out_v[t] = (part_own[t] + part_in[t].astype(F32)).astype(BF16)
        store = pltpu.make_async_copy(
            out_v.at[t], out_hbm.at[pl.ds(t * LANE, LANE)], store_sem.at[t]
        )
        store.start()
        stores.append(store)

    for store in stores:
        store.wait()
    for i, (src, dst) in enumerate([(send_f, recv_f), (send_s, recv_s), (send_c, recv_c)]):
        a2a_all(i, src, dst).wait_send()
    for copy in near_copies + [spread_all, to_sibling] + swaps + parts:
        copy.wait_send()


def per_device(query_proj, key_proj, value_proj, filter_taps, skip_gain, out_weight):
    blocks = lax.axis_size("ctx")
    rows, width = query_proj.shape
    group = width // blocks
    sub = rows // LANE
    half = blocks * sub
    tables = [jnp.asarray(t) for t in dft_tables(blocks, rows)]
    gain = skip_gain[None, :]
    dma = pltpu.SemaphoreType.DMA

    def like(x):
        return pltpu.VMEM(x.shape, x.dtype)

    flat = pltpu.VMEM((width, rows), BF16)
    wide = pltpu.VMEM((sub, width, LANE), F32)
    weights = pltpu.VMEM((width, 2 * width), BF16)
    piece = pltpu.VMEM((sub, LANE, width), BF16)
    return pl.pallas_call(
        functools.partial(whole_kernel, blocks, group, sub, width),
        out_shape=jax.ShapeDtypeStruct((rows, width), BF16),
        in_specs=[pl.BlockSpec(memory_space=pl.ANY)] * (6 + len(tables)),
        out_specs=pl.BlockSpec(memory_space=pl.ANY),
        scratch_shapes=[
            like(query_proj), like(key_proj), like(value_proj), like(filter_taps), like(gain),
            weights, weights,
            *[like(t) for t in tables],
            *[flat] * 6,
            wide, wide, pltpu.VMEM((group, half, 2 * LANE), F32),
            piece, piece, piece, piece, pltpu.VMEM((sub, LANE, width), F32), piece,
            dma((7,)), dma((len(tables),)), dma((3,)), dma((sub,)),
            dma((3,)), dma((3,)), dma((2,)), dma((2,)), dma, dma, dma, dma,
            dma((sub,)), dma((sub,)), dma((sub,)), dma((sub,)),
        ],
        compiler_params=pltpu.CompilerParams(
            collective_id=0, has_side_effects=True, vmem_limit_bytes=56 * 1024 * 1024
        ),
    )(query_proj, key_proj, value_proj, filter_taps, gain, out_weight, *tables)


def solution(mesh):
    placed = (
        P("ctx", "chan"),
        P("ctx", "chan"),
        P("ctx", "chan"),
        P("ctx", "chan"),
        P("chan"),
        P("chan", None),
    )
    return jax.shard_map(
        per_device, mesh=mesh, in_specs=placed, out_specs=P("ctx", "chan"), check_vma=False
    )
```

```python
import functools
import math

import jax
import jax.numpy as jnp
import numpy as np
import ml_dtypes
from jax import lax
from jax.experimental import pallas as pl
from jax.experimental.pallas import tpu as pltpu
from jax.sharding import PartitionSpec as P

BF16 = jnp.bfloat16
F32 = jnp.float32
LANE = 128


def split_const(table):
    high = table.astype(np.float32).astype(ml_dtypes.bfloat16)
    low = (table - high.astype(np.float64)).astype(np.float32).astype(ml_dtypes.bfloat16)
    return high, low


def dft_tables(chips, runs):
    sub = 2 * runs
    half = chips * sub
    outer = 2 * half
    full = outer * LANE
    run, core, chip = np.meshgrid(np.arange(runs), np.arange(2), np.arange(chips), indexing="ij")
    order = (chip * sub + core * runs + run).reshape(-1)
    freq = np.arange(half) + 0.5
    phase = 2.0 * math.pi * ((order[None, :] * (2 * np.arange(half)[:, None] + 1)) % (2 * outer)) / (2 * outer)
    first = np.concatenate([np.cos(phase), -np.sin(phase)], 0)
    back = np.concatenate([np.cos(phase).T, -np.sin(phase).T], 1) * (2.0 / full)
    turn = 2.0 * math.pi * np.arange(LANE)[None, :] * freq[:, None] / full
    inner = 2.0 * math.pi * ((np.arange(LANE)[:, None] * np.arange(LANE)[None, :]) % LANE) / LANE
    c, s = np.cos(inner), np.sin(inner)
    forward = np.block([[c, -s], [s, c]])
    inverse = np.block([[c, s], [-s, c]])
    return (
        *split_const(first),
        *split_const(forward),
        *split_const(inverse),
        *split_const(back),
        np.cos(turn).astype(np.float32),
        np.sin(turn).astype(np.float32),
    )


def dot(a, b):
    return jnp.dot(a, b, preferred_element_type=F32)


def split(x):
    high = x.astype(BF16)
    low = (x - high.astype(F32)).astype(BF16)
    return high, low


def dot3(x, m_hi, m_lo):
    hi, lo = split(x)
    return dot(hi, m_hi) + dot(lo, m_hi) + dot(hi, m_lo)


MESH = pl.DeviceIdType.MESH
COLS = 256
SETS = 2
PART = 8


def whole_kernel(
    chips, runs, width,
    q_hbm, k_hbm, v_hbm, f_hbm, gain_hbm, w_hbm,
    first_hi, first_lo, fw_hi_in, fw_lo_in, iv_hi_in, iv_lo_in, bk_hi_in, bk_lo_in, cos_in, sin_in,
    out_hbm,
    q_v, k_v, v_v, f_v, gain_v, w_own, w_near,
    a_hi, a_lo, fw_hi, fw_lo, iv_hi, iv_lo, bk_hi, bk_lo, cos_ref, sin_ref,
    keep_f, keep_s, give_f, give_s, give_c, take_f, take_s, take_c,
    send_f, send_s, send_c, recv_f, recv_s, recv_c,
    wide_a, wide_b, spec_f,
    g_own, g_near, part_out, part_in, part_own, out_v,
    load_sem, table_sem, own_sem, store_sem,
    a2a_send, a2a_recv, x_send, x_recv, wz_send, wz_recv, wx_send, wx_recv, wc_send, wc_recv,
    g_send, g_recv, p_send, p_recv,
):
    c = lax.axis_index("ctx")
    h = lax.axis_index("chan")
    near = h + 1 - 2 * lax.rem(h, 2)
    far = lax.rem(h + 2, 4)
    far_near = lax.rem(near + 2, 4)
    core = lax.rem(c, 2)
    chip = lax.div(c, 2)
    sibling = c + 1 - 2 * core
    plane = lax.rem(c, 4)
    spot = lax.div(c, 4)
    spots = chips // 2
    half = chips * runs * 2
    side = width // 2
    tall = runs * 2 * PART
    slab = side // spots

    bar = pltpu.get_barrier_semaphore()

    def peer(j):
        return lax.rem(chip + j, chips) * 2 + core

    def greet(j, _):
        pl.semaphore_signal(bar, inc=1, device_id=(peer(j), h), device_id_type=MESH)
        return 0

    def block_cols(block):
        return pl.ds(pl.multiple_of(block * width, width), width)

    loads = [
        pltpu.make_async_copy(src, dst, load_sem.at[i])
        for i, (src, dst) in enumerate(
            [
                (f_hbm, f_v),
                (k_hbm, k_v),
                (v_hbm, v_v),
                (q_hbm, q_v),
                (gain_hbm, gain_v),
                (w_hbm.at[:, block_cols(h)], w_own.at[0]),
                (w_hbm.at[:, block_cols(far)], w_own.at[1]),
            ]
        )
    ]
    tables = [
        pltpu.make_async_copy(src, dst, table_sem.at[i])
        for i, (src, dst) in enumerate(
            zip(
                (first_hi, first_lo, fw_hi_in, fw_lo_in, iv_hi_in, iv_lo_in, bk_hi_in, bk_lo_in, cos_in, sin_in),
                (a_hi, a_lo, fw_hi, fw_lo, iv_hi, iv_lo, bk_hi, bk_lo, cos_ref, sin_ref),
            )
        )
    ]
    for copy in loads[:3]:
        copy.start()
    lax.fori_loop(1, chips, greet, 0)
    pl.semaphore_signal(bar, inc=1, device_id=(sibling, h), device_id_type=MESH)
    for other in (near, far):
        pl.semaphore_signal(bar, inc=1, device_id=(c, other), device_id_type=MESH)
    for copy in loads[3:] + tables:
        copy.start()

    def remote(src, dst, send, recv, device):
        return pltpu.make_async_remote_copy(
            src_ref=src, dst_ref=dst, send_sem=send, recv_sem=recv,
            device_id=device, device_id_type=MESH,
        )

    moves = [(send_f, recv_f, slice(0, SETS), (0, tall))]
    moves += [(send_s, recv_s, slice(g, g + 1), (0, tall)) for g in range(SETS)]
    moves += [(send_c, recv_c, slice(0, 1), (0, tall))]
    moves += [(send_c, recv_c, slice(1, 2), (a * 2 * PART, 2 * PART)) for a in range(runs)]

    def view(ref, i, first, count):
        _, _, sets, (start, size) = moves[i]
        return ref.at[sets, pl.ds(first, count), pl.ds(start, size), :]

    def a2a_own(i):
        src, dst = moves[i][:2]
        return pltpu.make_async_copy(view(src, i, chip, 1), view(dst, i, chip, 1), own_sem.at[i])

    def a2a_start(i):
        src, dst = moves[i][:2]

        def send(j, _):
            to = peer(j)
            remote(
                view(src, i, lax.rem(chip + j, chips), 1), view(dst, i, chip, 1),
                a2a_send.at[i], a2a_recv.at[i], (to, h),
            ).start()
            return 0

        a2a_own(i).start()
        lax.fori_loop(1, chips, send, 0)

    def a2a_all(i):
        src, dst = moves[i][:2]
        return remote(
            view(src, i, 0, chips - 1), view(dst, i, 0, chips - 1),
            a2a_send.at[i], a2a_recv.at[i], (sibling, h),
        )

    def a2a_arrived(i):
        a2a_own(i).wait()
        a2a_all(i).wait_recv()

    def swap_cores(i, src, dst):
        return remote(src, dst, x_send.at[i], x_recv.at[i], (sibling, h))

    mine = pl.multiple_of(core * side, side)
    theirs = pl.multiple_of(side - core * side, side)

    def turn(fetch, keep, give):
        for a in range(runs):
            here = slice(a * LANE, (a + 1) * LANE)
            for start, dst in ((theirs, give), (mine, keep)):
                for i in range(side // COLS):
                    cols = pl.ds(pl.multiple_of(start + i * COLS, COLS), COLS)
                    dst[a, i * COLS:(i + 1) * COLS, :] = fetch(here, cols).T.astype(BF16)

    def assemble(keep, take, dst):
        for a in range(runs):
            own = keep[a].astype(F32).reshape(chips, SETS, PART, LANE)
            got = take[a].astype(F32).reshape(chips, SETS, PART, LANE)
            for g in range(SETS):
                both = jnp.concatenate([own[:, g], got[:, g]], 1)
                dst[g, :, a * 2 * PART:(a + 1) * 2 * PART, :] = both.astype(BF16)

    loads[0].wait()
    turn(lambda here, cols: f_v[here, cols], keep_f, give_f)
    pl.semaphore_wait(bar, chips + 2)
    swap_f = swap_cores(0, give_f, take_f)
    swap_f.start()

    my_rows = pl.ds(pl.multiple_of(core * side + spot * slab, slab), slab)

    def near_slice(i, block):
        return remote(
            w_hbm.at[my_rows, block_cols(block)], w_near.at[i, my_rows],
            wz_send.at[i], wz_recv.at[i], (c, near),
        )

    near_copies = [near_slice(0, near), near_slice(1, far_near)]
    for copy in near_copies:
        copy.start()
    loads[1].wait()
    loads[2].wait()
    turn(
        lambda here, cols: k_v[here, cols].astype(F32) * v_v[here, cols].astype(F32), keep_s, give_s
    )
    swap_s = swap_cores(1, give_s, take_s)
    swap_s.start()
    swap_f.wait_recv()
    assemble(keep_f, take_f, send_f)
    a2a_start(0)
    swap_s.wait_recv()
    assemble(keep_s, take_s, send_s)
    for g in range(SETS):
        a2a_start(1 + g)

    def spread(i):
        def send(j, _):
            to = lax.rem(spot + j, spots) * 4 + plane
            remote(
                w_near.at[i, my_rows], w_near.at[i, my_rows], wx_send.at[i], wx_recv.at[i], (to, h)
            ).start()
            return 0

        near_copies[i].wait_recv()
        lax.fori_loop(1, spots, send, 0)

    def spread_all(i):
        most = pl.ds(0, (spots - 1) * slab)
        return remote(
            w_near.at[i, most], w_near.at[i, most], wx_send.at[i], wx_recv.at[i], (sibling, h)
        )

    def to_sibling(i):
        rows = pl.ds(mine, side)
        return remote(
            w_near.at[i, rows], w_near.at[i, rows], wc_send.at[i], wc_recv.at[i], (sibling, h)
        )

    spread(1)

    for copy in tables:
        copy.wait()

    def places(a, ch, at):
        return pl.ds(a * 2 * PART + lax.rem(core + at, 2) * PART + ch, chips, stride=tall)

    def columns(wide, ch):
        parts = [wide[places(a, ch, at), :] for a in range(runs) for at in range(2)]
        return jnp.concatenate(parts, 0).astype(BF16)

    def spectra(wide, chans):
        x = jnp.concatenate([columns(wide, ch) for ch in chans], 1)
        y = dot(a_hi[...], x) + dot(a_lo[...], x)
        cos, sin = cos_ref[...], sin_ref[...]
        found = []
        for j in range(len(chans)):
            re = y[:half, j * LANE:(j + 1) * LANE]
            im = y[half:, j * LANE:(j + 1) * LANE]
            turned = jnp.concatenate([re * cos + im * sin, im * cos - re * sin], 1)
            found.append(dot3(turned, fw_hi[...], fw_lo[...]))
        return found

    def widen(src):
        wide_a[...] = src.astype(F32).reshape(chips * tall, LANE)

    a2a_arrived(0)
    for g in range(SETS):
        widen(recv_f[g])

        def taps_step(p, _, g=g):
            chans = (2 * p, 2 * p + 1)
            for ch, spec in zip(chans, spectra(wide_a, chans)):
                spec_f[g * PART + ch] = spec
            return 0

        lax.fori_loop(0, PART // 2, taps_step, 0)

    for g in range(SETS):
        a2a_arrived(1 + g)
        widen(recv_s[g])

        def conv_step(p, _, g=g):
            chans = (2 * p, 2 * p + 1)
            cos, sin = cos_ref[...], sin_ref[...]
            backs = []
            for ch, s in zip(chans, spectra(wide_a, chans)):
                f = spec_f[g * PART + ch]
                s_re, s_im, f_re, f_im = s[:, :LANE], s[:, LANE:], f[:, :LANE], f[:, LANE:]
                product = jnp.concatenate([s_re * f_re - s_im * f_im, s_re * f_im + s_im * f_re], 1)
                z = dot3(product, iv_hi[...], iv_lo[...])
                re, im = z[:, :LANE], z[:, LANE:]
                backs.append(jnp.concatenate([re * cos - im * sin, im * cos + re * sin], 0))
            z_hi, z_lo = split(jnp.concatenate(backs, 1))
            res = dot(bk_hi[...], z_hi) + dot(bk_hi[...], z_lo) + dot(bk_lo[...], z_hi)
            for j, ch in enumerate(chans):
                for a in range(runs):
                    for at in range(2):
                        row = (2 * a + at) * chips
                        wide_b[places(a, ch, at), :] = res[
                            row:row + chips, j * LANE:(j + 1) * LANE
                        ]
            return 0

        lax.fori_loop(0, PART // 2, conv_step, 0)
        send_c[g] = wide_b[...].reshape(chips, tall, LANE).astype(BF16)
        for i in (range(3, 4) if g == 0 else range(4, 4 + runs)):
            a2a_start(i)

    spread_all(1).wait_recv()
    to_sibling(1).start()
    for copy in loads[3:]:
        copy.wait()

    def gated(a, conv, start):
        here = slice(a * LANE, (a + 1) * LANE)
        for i in range(side // COLS):
            cols = pl.ds(pl.multiple_of(start + i * COLS, COLS), COLS)
            signal = k_v[here, cols].astype(F32) * v_v[here, cols].astype(F32)
            turned = conv[i * COLS:(i + 1) * COLS, :].T
            g_own[a, :, cols] = (
                q_v[here, cols].astype(F32) * (turned + gain_v[:, cols] * signal)
            ).astype(BF16)

    a2a_arrived(3)
    swaps = []
    backs = []
    for a in range(runs):
        a2a_arrived(4 + a)
        tile = [recv_c[g, :, a * 2 * PART:(a + 1) * 2 * PART, :].astype(F32) for g in range(SETS)]
        other = jnp.concatenate([t[:, PART:] for t in tile], 1).reshape(side, LANE)
        give_c[a] = other.astype(BF16)
        back = swap_cores(2 + a, give_c.at[a], take_c.at[a])
        back.start()
        backs.append(back)
        own = jnp.concatenate([t[:, :PART] for t in tile], 1).reshape(side, LANE)
        gated(a, own, mine)
        back.wait_recv()
        gated(a, take_c[a].astype(F32), theirs)
        swap = remote(g_own.at[a], g_near.at[a], g_send.at[a], g_recv.at[a], (c, near))
        swap.start()
        swaps.append(swap)

    spread(0)

    def product(i, a, piece):
        cols = pl.ds(pl.multiple_of(piece * COLS, COLS), COLS)
        return cols, dot(g_own[a], w_own[i, :, cols]) + dot(g_near[a], w_near[i, :, cols])

    to_sibling(1).wait_recv()
    parts = []
    for a in range(runs):
        swaps[a].wait_recv()

        def project(piece, _, a=a):
            cols, sums = product(1, a, piece)
            part_out[a, :, cols] = sums.astype(BF16)
            return 0

        lax.fori_loop(0, width // COLS, project, 0)
        part = remote(part_out.at[a], part_in.at[a], p_send.at[a], p_recv.at[a], (c, far))
        part.start()
        parts.append(part)
    spread_all(0).wait_recv()
    to_sibling(0).start()
    to_sibling(0).wait_recv()
    for a in range(runs):

        def project_own(piece, _, a=a):
            cols, sums = product(0, a, piece)
            part_own[a, :, cols] = sums
            return 0

        lax.fori_loop(0, width // COLS, project_own, 0)
    stores = []
    for a in range(runs):
        parts[a].wait_recv()
        out_v[a] = (part_own[a] + part_in[a].astype(F32)).astype(BF16)
        store = pltpu.make_async_copy(
            out_v.at[a], out_hbm.at[pl.ds(a * LANE, LANE)], store_sem.at[a]
        )
        store.start()
        stores.append(store)

    for store in stores:
        store.wait()
    for i in range(len(moves)):
        a2a_all(i).wait_send()
    for i in range(2):
        spread_all(i).wait_send()
        to_sibling(i).wait_send()
    for copy in near_copies + [swap_f, swap_s] + backs + swaps + parts:
        copy.wait_send()


def per_device(query_proj, key_proj, value_proj, filter_taps, skip_gain, out_weight):
    chips = lax.axis_size("ctx") // 2
    rows, width = query_proj.shape
    runs = rows // LANE
    side = width // 2
    half = chips * runs * 2
    tables = [jnp.asarray(t) for t in dft_tables(chips, runs)]
    gain = skip_gain[None, :]
    dma = pltpu.SemaphoreType.DMA

    def like(x):
        return pltpu.VMEM(x.shape, x.dtype)

    tall = runs * 2 * PART
    flat = pltpu.VMEM((SETS, chips, tall, LANE), BF16)
    swapped = pltpu.VMEM((runs, side, LANE), BF16)
    wide = pltpu.VMEM((chips * tall, LANE), F32)
    weights = pltpu.VMEM((2, width, width), BF16)
    piece = pltpu.VMEM((runs, LANE, width), BF16)
    moves = 1 + SETS + 1 + runs
    return pl.pallas_call(
        functools.partial(whole_kernel, chips, runs, width),
        out_shape=jax.ShapeDtypeStruct((rows, width), BF16),
        in_specs=[pl.BlockSpec(memory_space=pl.ANY)] * (6 + len(tables)),
        out_specs=pl.BlockSpec(memory_space=pl.ANY),
        scratch_shapes=[
            like(query_proj), like(key_proj), like(value_proj), like(filter_taps), like(gain),
            weights, weights,
            *[like(t) for t in tables],
            *[swapped] * 8,
            *[flat] * 6,
            wide, wide, pltpu.VMEM((SETS * PART, half, 2 * LANE), F32),
            piece, piece, piece, piece, pltpu.VMEM((runs, LANE, width), F32), piece,
            dma((7,)), dma((len(tables),)), dma((moves,)), dma((runs,)),
            dma((moves,)), dma((moves,)), dma((2 + runs,)), dma((2 + runs,)),
            dma((2,)), dma((2,)), dma((2,)), dma((2,)), dma((2,)), dma((2,)),
            dma((runs,)), dma((runs,)), dma((runs,)), dma((runs,)),
        ],
        compiler_params=pltpu.CompilerParams(
            collective_id=0, has_side_effects=True, vmem_limit_bytes=56 * 1024 * 1024
        ),
    )(query_proj, key_proj, value_proj, filter_taps, gain, out_weight, *tables)


def solution(mesh):
    placed = (
        P("ctx", "chan"),
        P("ctx", "chan"),
        P("ctx", "chan"),
        P("ctx", "chan"),
        P("chan"),
        P("chan", None),
    )
    return jax.shard_map(
        per_device, mesh=mesh, in_specs=placed, out_specs=P("ctx", "chan"), check_vma=False
    )
```

```python
import functools
import math

import jax
import jax.numpy as jnp
import numpy as np
import ml_dtypes
from jax import lax
from jax.experimental import pallas as pl
from jax.experimental.pallas import tpu as pltpu
from jax.sharding import PartitionSpec as P

BF16 = jnp.bfloat16
F32 = jnp.float32
LANE = 128


def split_const(table):
    high = table.astype(np.float32).astype(ml_dtypes.bfloat16)
    low = (table - high.astype(np.float64)).astype(np.float32).astype(ml_dtypes.bfloat16)
    return high, low


def dft_tables(chips, runs):
    sub = 2 * runs
    half = chips * sub
    outer = 2 * half
    full = outer * LANE
    run, core, chip = np.meshgrid(np.arange(runs), np.arange(2), np.arange(chips), indexing="ij")
    order = (chip * sub + core * runs + run).reshape(-1)
    freq = np.arange(half) + 0.5
    phase = 2.0 * math.pi * ((order[None, :] * (2 * np.arange(half)[:, None] + 1)) % (2 * outer)) / (2 * outer)
    first = np.concatenate([np.cos(phase), -np.sin(phase)], 0)
    back = np.concatenate([np.cos(phase).T, -np.sin(phase).T], 1) * (2.0 / full)
    turn = 2.0 * math.pi * np.arange(LANE)[None, :] * freq[:, None] / full
    inner = 2.0 * math.pi * ((np.arange(LANE)[:, None] * np.arange(LANE)[None, :]) % LANE) / LANE
    c, s = np.cos(inner), np.sin(inner)
    forward = np.block([[c, -s], [s, c]])
    inverse = np.block([[c, s], [-s, c]])
    return (
        *split_const(first),
        *split_const(forward),
        *split_const(inverse),
        *split_const(back),
        np.cos(turn).astype(np.float32),
        np.sin(turn).astype(np.float32),
    )


def dot(a, b):
    return jnp.dot(a, b, preferred_element_type=F32)


def split(x):
    high = x.astype(BF16)
    low = (x - high.astype(F32)).astype(BF16)
    return high, low


def dot3(x, m_hi, m_lo):
    hi, lo = split(x)
    count = x.shape[0]
    both = dot(jnp.concatenate([hi, lo], 0), m_hi)
    return both[:count] + both[count:] + dot(hi, m_lo)


MESH = pl.DeviceIdType.MESH
COLS = 256
SETS = 2
PART = 8
PIECES = 2


def whole_kernel(
    chips, runs, width,
    q_hbm, k_hbm, v_hbm, f_hbm, gain_hbm, w_hbm,
    first_hi, first_lo, fw_hi_in, fw_lo_in, iv_hi_in, iv_lo_in, bk_hi_in, bk_lo_in, cos_in, sin_in,
    out_hbm,
    q_v, k_v, v_v, f_v, gain_v, w_own, w_near,
    a_hi, a_lo, fw_hi, fw_lo, iv_hi, iv_lo, bk_hi, bk_lo, cos_ref, sin_ref,
    keep_f, keep_s, give_f, give_s, give_c, take_f, take_s, take_c,
    send_f, send_s, send_c, recv_f, recv_s, recv_c,
    wide_a, wide_b, spec_f,
    g_own, g_near, part_out, part_in, part_own, out_v,
    load_sem, table_sem, own_sem, store_sem,
    a2a_send, a2a_recv, x_send, x_recv, wz_send, wz_recv, wx_send, wx_recv, wc_send, wc_recv,
    g_send, g_recv, p_send, p_recv,
):
    c = lax.axis_index("ctx")
    h = lax.axis_index("chan")
    near = h + 1 - 2 * lax.rem(h, 2)
    far = lax.rem(h + 2, 4)
    far_near = lax.rem(near + 2, 4)
    core = lax.rem(c, 2)
    chip = lax.div(c, 2)
    sibling = c + 1 - 2 * core
    plane = lax.rem(c, 4)
    spot = lax.div(c, 4)
    spots = chips // 2
    half = chips * runs * 2
    side = width // 2
    tall = runs * 2 * PART
    slab = side // spots

    bar = pltpu.get_barrier_semaphore()

    def peer(j):
        return lax.rem(chip + j, chips) * 2 + core

    def greet(j, _):
        pl.semaphore_signal(bar, inc=1, device_id=(peer(j), h), device_id_type=MESH)
        return 0

    def block_cols(block):
        return pl.ds(pl.multiple_of(block * width, width), width)

    loads = [
        pltpu.make_async_copy(src, dst, load_sem.at[i])
        for i, (src, dst) in enumerate(
            [
                (f_hbm, f_v),
                (k_hbm, k_v),
                (v_hbm, v_v),
                (q_hbm, q_v),
                (gain_hbm, gain_v),
                (w_hbm.at[:, block_cols(h)], w_own.at[0]),
                (w_hbm.at[:, block_cols(far)], w_own.at[1]),
            ]
        )
    ]
    tables = [
        pltpu.make_async_copy(src, dst, table_sem.at[i])
        for i, (src, dst) in enumerate(
            zip(
                (first_hi, first_lo, fw_hi_in, fw_lo_in, iv_hi_in, iv_lo_in, bk_hi_in, bk_lo_in, cos_in, sin_in),
                (a_hi, a_lo, fw_hi, fw_lo, iv_hi, iv_lo, bk_hi, bk_lo, cos_ref, sin_ref),
            )
        )
    ]
    for copy in loads[:3]:
        copy.start()
    lax.fori_loop(1, chips, greet, 0)
    pl.semaphore_signal(bar, inc=1, device_id=(sibling, h), device_id_type=MESH)
    for other in (near, far):
        pl.semaphore_signal(bar, inc=1, device_id=(c, other), device_id_type=MESH)
    for copy in loads[3:] + tables:
        copy.start()

    def remote(src, dst, send, recv, device):
        return pltpu.make_async_remote_copy(
            src_ref=src, dst_ref=dst, send_sem=send, recv_sem=recv,
            device_id=device, device_id_type=MESH,
        )

    moves = [(send_f, recv_f, slice(0, SETS), (0, tall))]
    moves += [(send_s, recv_s, slice(g, g + 1), (0, tall)) for g in range(SETS)]
    moves += [(send_c, recv_c, slice(0, 1), (0, tall))]
    moves += [(send_c, recv_c, slice(1, 2), (a * 2 * PART, 2 * PART)) for a in range(runs)]

    def view(ref, i, first, count):
        _, _, sets, (start, size) = moves[i]
        return ref.at[sets, pl.ds(first, count), pl.ds(start, size), :]

    def a2a_own(i):
        src, dst = moves[i][:2]
        return pltpu.make_async_copy(view(src, i, chip, 1), view(dst, i, chip, 1), own_sem.at[i])

    def a2a_start(i):
        src, dst = moves[i][:2]

        def send(j, _):
            to = peer(j)
            remote(
                view(src, i, lax.rem(chip + j, chips), 1), view(dst, i, chip, 1),
                a2a_send.at[i], a2a_recv.at[i], (to, h),
            ).start()
            return 0

        a2a_own(i).start()
        lax.fori_loop(1, chips, send, 0)

    def a2a_all(i):
        src, dst = moves[i][:2]
        return remote(
            view(src, i, 0, chips - 1), view(dst, i, 0, chips - 1),
            a2a_send.at[i], a2a_recv.at[i], (sibling, h),
        )

    def a2a_arrived(i):
        a2a_own(i).wait()
        a2a_all(i).wait_recv()

    def swap_cores(i, src, dst):
        return remote(src, dst, x_send.at[i], x_recv.at[i], (sibling, h))

    mine = pl.multiple_of(core * side, side)
    theirs = pl.multiple_of(side - core * side, side)

    def turn(fetch, keep, give):
        for a in range(runs):
            here = slice(a * LANE, (a + 1) * LANE)
            for start, dst in ((theirs, give), (mine, keep)):
                for i in range(side // COLS):
                    cols = pl.ds(pl.multiple_of(start + i * COLS, COLS), COLS)
                    dst[a, i * COLS:(i + 1) * COLS, :] = fetch(here, cols).T.astype(BF16)

    def assemble(keep, take, dst):
        for a in range(runs):
            own = keep[a].astype(F32).reshape(chips, SETS, PART, LANE)
            got = take[a].astype(F32).reshape(chips, SETS, PART, LANE)
            for g in range(SETS):
                both = jnp.concatenate([own[:, g], got[:, g]], 1)
                dst[g, :, a * 2 * PART:(a + 1) * 2 * PART, :] = both.astype(BF16)

    loads[0].wait()
    turn(lambda here, cols: f_v[here, cols], keep_f, give_f)
    pl.semaphore_wait(bar, chips + 2)
    swap_f = swap_cores(0, give_f, take_f)
    swap_f.start()

    my_rows = pl.ds(pl.multiple_of(core * side + spot * slab, slab), slab)

    def near_slice(i, block):
        return remote(
            w_hbm.at[my_rows, block_cols(block)], w_near.at[i, my_rows],
            wz_send.at[i], wz_recv.at[i], (c, near),
        )

    near_copies = [near_slice(0, near), near_slice(1, far_near)]
    for copy in near_copies:
        copy.start()
    loads[1].wait()
    loads[2].wait()
    turn(
        lambda here, cols: k_v[here, cols].astype(F32) * v_v[here, cols].astype(F32), keep_s, give_s
    )
    swap_s = swap_cores(1, give_s, take_s)
    swap_s.start()
    swap_f.wait_recv()
    assemble(keep_f, take_f, send_f)
    a2a_start(0)
    swap_s.wait_recv()
    assemble(keep_s, take_s, send_s)
    for g in range(SETS):
        a2a_start(1 + g)

    def spread(i):
        def send(j, _):
            to = lax.rem(spot + j, spots) * 4 + plane
            remote(
                w_near.at[i, my_rows], w_near.at[i, my_rows], wx_send.at[i], wx_recv.at[i], (to, h)
            ).start()
            return 0

        near_copies[i].wait_recv()
        lax.fori_loop(1, spots, send, 0)

    def spread_all(i):
        most = pl.ds(0, (spots - 1) * slab)
        return remote(
            w_near.at[i, most], w_near.at[i, most], wx_send.at[i], wx_recv.at[i], (sibling, h)
        )

    def to_sibling(i):
        rows = pl.ds(mine, side)
        return remote(
            w_near.at[i, rows], w_near.at[i, rows], wc_send.at[i], wc_recv.at[i], (sibling, h)
        )

    spread(1)

    for copy in tables:
        copy.wait()

    def places(a, ch, at):
        return pl.ds(a * 2 * PART + lax.rem(core + at, 2) * PART + ch, chips, stride=tall)

    def columns(wide, ch):
        parts = [wide[places(a, ch, at), :] for a in range(runs) for at in range(2)]
        return jnp.concatenate(parts, 0).astype(BF16)

    def spectra(wide, chans):
        x = jnp.concatenate([columns(wide, ch) for ch in chans], 1)
        y = dot(a_hi[...], x) + dot(a_lo[...], x)
        cos, sin = cos_ref[...], sin_ref[...]
        found = []
        for j in range(len(chans)):
            re = y[:half, j * LANE:(j + 1) * LANE]
            im = y[half:, j * LANE:(j + 1) * LANE]
            turned = jnp.concatenate([re * cos + im * sin, im * cos - re * sin], 1)
            found.append(turned)
        spec = dot3(jnp.concatenate(found, 0), fw_hi[...], fw_lo[...])
        return [spec[j * half:(j + 1) * half] for j in range(len(chans))]

    def widen(src):
        wide_a[...] = src.astype(F32).reshape(chips * tall, LANE)

    a2a_arrived(0)
    for g in range(SETS):
        widen(recv_f[g])

        def taps_step(p, _, g=g):
            chans = (2 * p, 2 * p + 1)
            for ch, spec in zip(chans, spectra(wide_a, chans)):
                spec_f[g * PART + ch] = spec
            return 0

        lax.fori_loop(0, PART // 2, taps_step, 0)

    for g in range(SETS):
        a2a_arrived(1 + g)
        widen(recv_s[g])

        def conv_step(p, _, g=g):
            chans = (2 * p, 2 * p + 1)
            cos, sin = cos_ref[...], sin_ref[...]
            backs = []
            products = []
            for ch, s in zip(chans, spectra(wide_a, chans)):
                f = spec_f[g * PART + ch]
                s_re, s_im, f_re, f_im = s[:, :LANE], s[:, LANE:], f[:, :LANE], f[:, LANE:]
                products.append(
                    jnp.concatenate([s_re * f_re - s_im * f_im, s_re * f_im + s_im * f_re], 1)
                )
            back = dot3(jnp.concatenate(products, 0), iv_hi[...], iv_lo[...])
            for j in range(len(chans)):
                z = back[j * half:(j + 1) * half]
                re, im = z[:, :LANE], z[:, LANE:]
                backs.append(jnp.concatenate([re * cos - im * sin, im * cos + re * sin], 0))
            z_hi, z_lo = split(jnp.concatenate(backs, 1))
            res = dot(bk_hi[...], z_hi) + dot(bk_hi[...], z_lo) + dot(bk_lo[...], z_hi)
            for j, ch in enumerate(chans):
                for a in range(runs):
                    for at in range(2):
                        row = (2 * a + at) * chips
                        wide_b[places(a, ch, at), :] = res[
                            row:row + chips, j * LANE:(j + 1) * LANE
                        ]
            return 0

        lax.fori_loop(0, PART // 2, conv_step, 0)
        send_c[g] = wide_b[...].reshape(chips, tall, LANE).astype(BF16)
        for i in (range(3, 4) if g == 0 else range(4, 4 + runs)):
            a2a_start(i)

    spread_all(1).wait_recv()
    to_sibling(1).start()
    for copy in loads[3:]:
        copy.wait()

    def gated(a, conv, start):
        here = slice(a * LANE, (a + 1) * LANE)
        for i in range(side // COLS):
            cols = pl.ds(pl.multiple_of(start + i * COLS, COLS), COLS)
            signal = k_v[here, cols].astype(F32) * v_v[here, cols].astype(F32)
            turned = conv[i * COLS:(i + 1) * COLS, :].T
            g_own[a, :, cols] = (
                q_v[here, cols].astype(F32) * (turned + gain_v[:, cols] * signal)
            ).astype(BF16)

    a2a_arrived(3)
    swaps = []
    backs = []
    parts = []
    step = LANE // PIECES

    def gate_run(a):
        a2a_arrived(4 + a)
        tile = [recv_c[g, :, a * 2 * PART:(a + 1) * 2 * PART, :].astype(F32) for g in range(SETS)]
        other = jnp.concatenate([t[:, PART:] for t in tile], 1).reshape(side, LANE)
        give_c[a] = other.astype(BF16)
        back = swap_cores(2 + a, give_c.at[a], take_c.at[a])
        back.start()
        backs.append(back)
        own = jnp.concatenate([t[:, :PART] for t in tile], 1).reshape(side, LANE)
        gated(a, own, mine)
        back.wait_recv()
        gated(a, take_c[a].astype(F32), theirs)
        for b in range(PIECES):
            i = a * PIECES + b
            here = pl.ds(b * step, step)
            swap = remote(
                g_own.at[a, here], g_near.at[a, here], g_send.at[i], g_recv.at[i], (c, near)
            )
            swap.start()
            swaps.append(swap)

    def product(i, a, here, piece):
        cols = pl.ds(pl.multiple_of(piece * COLS, COLS), COLS)
        return cols, dot(g_own[a, here], w_own[i, :, cols]) + dot(g_near[a, here], w_near[i, :, cols])

    def project_run(a):
        for b in range(PIECES):
            i = a * PIECES + b
            here = slice(b * step, (b + 1) * step)
            swaps[i].wait_recv()

            def project(piece, _):
                cols, sums = product(1, a, here, piece)
                part_out[a, here, cols] = sums.astype(BF16)
                return 0

            lax.fori_loop(0, width // COLS, project, 0)
            rows = pl.ds(b * step, step)
            part = remote(
                part_out.at[a, rows], part_in.at[a, rows], p_send.at[i], p_recv.at[i], (c, far)
            )
            part.start()
            parts.append(part)

    for a in range(runs):
        gate_run(a)
        if a == runs - 1:
            spread(0)
        if a == 0:
            to_sibling(1).wait_recv()
        else:
            project_run(a - 1)
    project_run(runs - 1)
    spread_all(0).wait_recv()
    to_sibling(0).start()
    to_sibling(0).wait_recv()
    for a in range(runs):

        def project_own(piece, _, a=a):
            cols, sums = product(0, a, slice(None), piece)
            part_own[a, :, cols] = sums
            return 0

        lax.fori_loop(0, width // COLS, project_own, 0)
    stores = []
    for a in range(runs):
        for b in range(PIECES):
            i = a * PIECES + b
            here = slice(b * step, (b + 1) * step)
            parts[i].wait_recv()
            out_v[a, here] = (part_own[a, here] + part_in[a, here].astype(F32)).astype(BF16)
            store = pltpu.make_async_copy(
                out_v.at[a, pl.ds(b * step, step)],
                out_hbm.at[pl.ds(a * LANE + b * step, step)],
                store_sem.at[i],
            )
            store.start()
            stores.append(store)

    for store in stores:
        store.wait()
    for i in range(len(moves)):
        a2a_all(i).wait_send()
    for i in range(2):
        spread_all(i).wait_send()
        to_sibling(i).wait_send()
    for copy in near_copies + [swap_f, swap_s] + backs + swaps + parts:
        copy.wait_send()


def per_device(query_proj, key_proj, value_proj, filter_taps, skip_gain, out_weight):
    chips = lax.axis_size("ctx") // 2
    rows, width = query_proj.shape
    runs = rows // LANE
    side = width // 2
    half = chips * runs * 2
    tables = [jnp.asarray(t) for t in dft_tables(chips, runs)]
    gain = skip_gain[None, :]
    dma = pltpu.SemaphoreType.DMA

    def like(x):
        return pltpu.VMEM(x.shape, x.dtype)

    tall = runs * 2 * PART
    flat = pltpu.VMEM((SETS, chips, tall, LANE), BF16)
    swapped = pltpu.VMEM((runs, side, LANE), BF16)
    wide = pltpu.VMEM((chips * tall, LANE), F32)
    weights = pltpu.VMEM((2, width, width), BF16)
    piece = pltpu.VMEM((runs, LANE, width), BF16)
    moves = 1 + SETS + 1 + runs
    return pl.pallas_call(
        functools.partial(whole_kernel, chips, runs, width),
        out_shape=jax.ShapeDtypeStruct((rows, width), BF16),
        in_specs=[pl.BlockSpec(memory_space=pl.ANY)] * (6 + len(tables)),
        out_specs=pl.BlockSpec(memory_space=pl.ANY),
        scratch_shapes=[
            like(query_proj), like(key_proj), like(value_proj), like(filter_taps), like(gain),
            weights, weights,
            *[like(t) for t in tables],
            *[swapped] * 8,
            *[flat] * 6,
            wide, wide, pltpu.VMEM((SETS * PART, half, 2 * LANE), F32),
            piece, piece, piece, piece, pltpu.VMEM((runs, LANE, width), F32), piece,
            dma((7,)), dma((len(tables),)), dma((moves,)), dma((runs * PIECES,)),
            dma((moves,)), dma((moves,)), dma((2 + runs,)), dma((2 + runs,)),
            dma((2,)), dma((2,)), dma((2,)), dma((2,)), dma((2,)), dma((2,)),
            *[dma((runs * PIECES,))] * 4,
        ],
        compiler_params=pltpu.CompilerParams(
            collective_id=0, has_side_effects=True, vmem_limit_bytes=56 * 1024 * 1024
        ),
    )(query_proj, key_proj, value_proj, filter_taps, gain, out_weight, *tables)


def solution(mesh):
    placed = (
        P("ctx", "chan"),
        P("ctx", "chan"),
        P("ctx", "chan"),
        P("ctx", "chan"),
        P("chan"),
        P("chan", None),
    )
    return jax.shard_map(
        per_device, mesh=mesh, in_specs=placed, out_specs=P("ctx", "chan"), check_vma=False
    )
```

```python
import functools
import math

import jax
import jax.numpy as jnp
import numpy as np
import ml_dtypes
from jax import lax
from jax.experimental import pallas as pl
from jax.experimental.pallas import tpu as pltpu
from jax.sharding import PartitionSpec as P

BF16 = jnp.bfloat16
F32 = jnp.float32
LANE = 128


def split_const(table):
    high = table.astype(np.float32).astype(ml_dtypes.bfloat16)
    low = (table - high.astype(np.float64)).astype(np.float32).astype(ml_dtypes.bfloat16)
    return high, low


def dft_tables(chips, runs):
    sub = 2 * runs
    half = chips * sub
    outer = 2 * half
    full = outer * LANE
    run, core, chip = np.meshgrid(np.arange(runs), np.arange(2), np.arange(chips), indexing="ij")
    order = (chip * sub + core * runs + run).reshape(-1)
    freq = np.arange(half) + 0.5
    phase = 2.0 * math.pi * ((order[None, :] * (2 * np.arange(half)[:, None] + 1)) % (2 * outer)) / (2 * outer)
    first = np.concatenate([np.cos(phase), -np.sin(phase)], 0)
    back = np.concatenate([np.cos(phase).T, -np.sin(phase).T], 1) * (2.0 / full)
    turn = 2.0 * math.pi * np.arange(LANE)[None, :] * freq[:, None] / full
    inner = 2.0 * math.pi * ((np.arange(LANE)[:, None] * np.arange(LANE)[None, :]) % LANE) / LANE
    c, s = np.cos(inner), np.sin(inner)
    forward = np.block([[c, -s], [s, c]])
    inverse = np.block([[c, s], [-s, c]])
    return (
        *split_const(first),
        *split_const(forward),
        *split_const(inverse),
        *split_const(back),
        np.cos(turn).astype(np.float32),
        np.sin(turn).astype(np.float32),
    )


def dot(a, b):
    return jnp.dot(a, b, preferred_element_type=F32)


def split(x):
    high = x.astype(BF16)
    low = (x - high.astype(F32)).astype(BF16)
    return high, low


def dot3(x, m_hi, m_lo):
    hi, lo = split(x)
    count = x.shape[0]
    both = dot(jnp.concatenate([hi, lo], 0), m_hi)
    return both[:count] + both[count:] + dot(hi, m_lo)


MESH = pl.DeviceIdType.MESH
COLS = 256
SETS = 2
PART = 8
PIECES = 4


def whole_kernel(
    chips, runs, width,
    q_hbm, k_hbm, v_hbm, f_hbm, gain_hbm, w_hbm,
    first_hi, first_lo, fw_hi_in, fw_lo_in, iv_hi_in, iv_lo_in, bk_hi_in, bk_lo_in, cos_in, sin_in,
    out_hbm,
    q_v, k_v, v_v, f_v, gain_v, w_own, w_near,
    a_hi, a_lo, fw_hi, fw_lo, iv_hi, iv_lo, bk_hi, bk_lo, cos_ref, sin_ref,
    keep_f, keep_s, give_f, give_s, give_c, take_f, take_s, take_c,
    send_f, send_s, send_c, recv_f, recv_s, recv_c,
    wide_a, wide_b, spec_f,
    g_own, g_near, part_out, part_in, part_own, out_v,
    load_sem, table_sem, own_sem, store_sem,
    a2a_send, a2a_recv, x_send, x_recv, wz_send, wz_recv, wx_send, wx_recv, wc_send, wc_recv,
    g_send, g_recv, p_send, p_recv,
):
    c = lax.axis_index("ctx")
    h = lax.axis_index("chan")
    near = h + 1 - 2 * lax.rem(h, 2)
    far = lax.rem(h + 2, 4)
    far_near = lax.rem(near + 2, 4)
    core = lax.rem(c, 2)
    chip = lax.div(c, 2)
    sibling = c + 1 - 2 * core
    plane = lax.rem(c, 4)
    spot = lax.div(c, 4)
    spots = chips // 2
    half = chips * runs * 2
    side = width // 2
    tall = runs * 2 * PART
    slab = side // spots

    bar = pltpu.get_barrier_semaphore()

    def peer(j):
        return lax.rem(chip + j, chips) * 2 + core

    def greet(j, _):
        pl.semaphore_signal(bar, inc=1, device_id=(peer(j), h), device_id_type=MESH)
        return 0

    def block_cols(block):
        return pl.ds(pl.multiple_of(block * width, width), width)

    loads = [
        pltpu.make_async_copy(src, dst, load_sem.at[i])
        for i, (src, dst) in enumerate(
            [
                (f_hbm, f_v),
                (k_hbm, k_v),
                (v_hbm, v_v),
                (q_hbm, q_v),
                (gain_hbm, gain_v),
                (w_hbm.at[:, block_cols(h)], w_own.at[0]),
                (w_hbm.at[:, block_cols(far)], w_own.at[1]),
            ]
        )
    ]
    tables = [
        pltpu.make_async_copy(src, dst, table_sem.at[i])
        for i, (src, dst) in enumerate(
            zip(
                (first_hi, first_lo, fw_hi_in, fw_lo_in, iv_hi_in, iv_lo_in, bk_hi_in, bk_lo_in, cos_in, sin_in),
                (a_hi, a_lo, fw_hi, fw_lo, iv_hi, iv_lo, bk_hi, bk_lo, cos_ref, sin_ref),
            )
        )
    ]
    for copy in loads[:3]:
        copy.start()
    lax.fori_loop(1, chips, greet, 0)
    pl.semaphore_signal(bar, inc=1, device_id=(sibling, h), device_id_type=MESH)
    for other in (near, far):
        pl.semaphore_signal(bar, inc=1, device_id=(c, other), device_id_type=MESH)
    for copy in loads[3:] + tables:
        copy.start()

    def remote(src, dst, send, recv, device):
        return pltpu.make_async_remote_copy(
            src_ref=src, dst_ref=dst, send_sem=send, recv_sem=recv,
            device_id=device, device_id_type=MESH,
        )

    moves = [(send_f, recv_f, slice(0, SETS), (0, tall))]
    moves += [(send_s, recv_s, slice(g, g + 1), (0, tall)) for g in range(SETS)]
    moves += [(send_c, recv_c, slice(0, 1), (0, tall))]
    moves += [(send_c, recv_c, slice(1, 2), (a * 2 * PART, 2 * PART)) for a in range(runs)]

    def view(ref, i, first, count):
        _, _, sets, (start, size) = moves[i]
        return ref.at[sets, pl.ds(first, count), pl.ds(start, size), :]

    def a2a_own(i):
        src, dst = moves[i][:2]
        return pltpu.make_async_copy(view(src, i, chip, 1), view(dst, i, chip, 1), own_sem.at[i])

    def a2a_start(i):
        src, dst = moves[i][:2]

        def send(j, _):
            to = peer(j)
            remote(
                view(src, i, lax.rem(chip + j, chips), 1), view(dst, i, chip, 1),
                a2a_send.at[i], a2a_recv.at[i], (to, h),
            ).start()
            return 0

        a2a_own(i).start()
        if i < 3:
            lax.fori_loop(1, chips, send, 0)
        else:
            lax.fori_loop(0, chips // 2, lambda j, _: send(2 * j + 1, 0), 0)
            lax.fori_loop(1, chips // 2, lambda j, _: send(2 * j, 0), 0)

    def a2a_all(i):
        src, dst = moves[i][:2]
        return remote(
            view(src, i, 0, chips - 1), view(dst, i, 0, chips - 1),
            a2a_send.at[i], a2a_recv.at[i], (sibling, h),
        )

    def a2a_arrived(i):
        a2a_own(i).wait()
        a2a_all(i).wait_recv()

    def swap_cores(i, src, dst):
        return remote(src, dst, x_send.at[i], x_recv.at[i], (sibling, h))

    mine = pl.multiple_of(core * side, side)
    theirs = pl.multiple_of(side - core * side, side)

    def turn(fetch, keep, give):
        for a in range(runs):
            here = slice(a * LANE, (a + 1) * LANE)
            for start, dst in ((theirs, give), (mine, keep)):
                for i in range(side // COLS):
                    cols = pl.ds(pl.multiple_of(start + i * COLS, COLS), COLS)
                    dst[a, i * COLS:(i + 1) * COLS, :] = fetch(here, cols).T.astype(BF16)

    def assemble(keep, take, dst):
        for a in range(runs):
            own = keep[a].astype(F32).reshape(chips, SETS, PART, LANE)
            got = take[a].astype(F32).reshape(chips, SETS, PART, LANE)
            for g in range(SETS):
                both = jnp.concatenate([own[:, g], got[:, g]], 1)
                dst[g, :, a * 2 * PART:(a + 1) * 2 * PART, :] = both.astype(BF16)

    loads[0].wait()
    turn(lambda here, cols: f_v[here, cols], keep_f, give_f)
    pl.semaphore_wait(bar, chips + 2)
    swap_f = swap_cores(0, give_f, take_f)
    swap_f.start()

    my_rows = pl.ds(pl.multiple_of(core * side + spot * slab, slab), slab)

    def near_slice(i, block):
        return remote(
            w_hbm.at[my_rows, block_cols(block)], w_near.at[i, my_rows],
            wz_send.at[i], wz_recv.at[i], (c, near),
        )

    near_copies = [near_slice(0, near), near_slice(1, far_near)]
    for copy in near_copies:
        copy.start()
    loads[1].wait()
    loads[2].wait()
    turn(
        lambda here, cols: k_v[here, cols].astype(F32) * v_v[here, cols].astype(F32), keep_s, give_s
    )
    swap_s = swap_cores(1, give_s, take_s)
    swap_s.start()
    swap_f.wait_recv()
    assemble(keep_f, take_f, send_f)
    a2a_start(0)
    swap_s.wait_recv()
    assemble(keep_s, take_s, send_s)
    for g in range(SETS):
        a2a_start(1 + g)

    def spread(i):
        def send(j, _):
            to = lax.rem(spot + j, spots) * 4 + plane
            remote(
                w_near.at[i, my_rows], w_near.at[i, my_rows], wx_send.at[i], wx_recv.at[i], (to, h)
            ).start()
            return 0

        near_copies[i].wait_recv()
        lax.fori_loop(1, spots, send, 0)

    def spread_all(i):
        most = pl.ds(0, (spots - 1) * slab)
        return remote(
            w_near.at[i, most], w_near.at[i, most], wx_send.at[i], wx_recv.at[i], (sibling, h)
        )

    def to_sibling(i):
        rows = pl.ds(mine, side)
        return remote(
            w_near.at[i, rows], w_near.at[i, rows], wc_send.at[i], wc_recv.at[i], (sibling, h)
        )

    spread(1)

    for copy in tables:
        copy.wait()

    def places(a, ch, at):
        return pl.ds(a * 2 * PART + lax.rem(core + at, 2) * PART + ch, chips, stride=tall)

    def columns(wide, ch):
        parts = [wide[places(a, ch, at), :] for a in range(runs) for at in range(2)]
        return jnp.concatenate(parts, 0).astype(BF16)

    def spectra(wide, chans):
        x = jnp.concatenate([columns(wide, ch) for ch in chans], 1)
        y = dot(a_hi[...], x) + dot(a_lo[...], x)
        cos, sin = cos_ref[...], sin_ref[...]
        found = []
        for j in range(len(chans)):
            re = y[:half, j * LANE:(j + 1) * LANE]
            im = y[half:, j * LANE:(j + 1) * LANE]
            turned = jnp.concatenate([re * cos + im * sin, im * cos - re * sin], 1)
            found.append(turned)
        spec = dot3(jnp.concatenate(found, 0), fw_hi[...], fw_lo[...])
        return [spec[j * half:(j + 1) * half] for j in range(len(chans))]

    def widen(src):
        wide_a[...] = src.astype(F32).reshape(chips * tall, LANE)

    a2a_arrived(0)
    for g in range(SETS):
        widen(recv_f[g])

        def taps_step(p, _, g=g):
            chans = (2 * p, 2 * p + 1)
            for ch, spec in zip(chans, spectra(wide_a, chans)):
                spec_f[g * PART + ch] = spec
            return 0

        lax.fori_loop(0, PART // 2, taps_step, 0)

    for g in range(SETS):
        a2a_arrived(1 + g)
        widen(recv_s[g])

        def conv_step(p, _, g=g):
            chans = (2 * p, 2 * p + 1)
            cos, sin = cos_ref[...], sin_ref[...]
            backs = []
            products = []
            for ch, s in zip(chans, spectra(wide_a, chans)):
                f = spec_f[g * PART + ch]
                s_re, s_im, f_re, f_im = s[:, :LANE], s[:, LANE:], f[:, :LANE], f[:, LANE:]
                products.append(
                    jnp.concatenate([s_re * f_re - s_im * f_im, s_re * f_im + s_im * f_re], 1)
                )
            back = dot3(jnp.concatenate(products, 0), iv_hi[...], iv_lo[...])
            for j in range(len(chans)):
                z = back[j * half:(j + 1) * half]
                re, im = z[:, :LANE], z[:, LANE:]
                backs.append(jnp.concatenate([re * cos - im * sin, im * cos + re * sin], 0))
            z_hi, z_lo = split(jnp.concatenate(backs, 1))
            res = dot(bk_hi[...], z_hi) + dot(bk_hi[...], z_lo) + dot(bk_lo[...], z_hi)
            for j, ch in enumerate(chans):
                for a in range(runs):
                    for at in range(2):
                        row = (2 * a + at) * chips
                        wide_b[places(a, ch, at), :] = res[
                            row:row + chips, j * LANE:(j + 1) * LANE
                        ]
            return 0

        lax.fori_loop(0, PART // 2, conv_step, 0)
        send_c[g] = wide_b[...].reshape(chips, tall, LANE).astype(BF16)
        for i in (range(3, 4) if g == 0 else range(4, 4 + runs)):
            a2a_start(i)

    spread_all(1).wait_recv()
    to_sibling(1).start()
    for copy in loads[3:]:
        copy.wait()

    def gated(a, conv, start):
        here = slice(a * LANE, (a + 1) * LANE)
        for i in range(side // COLS):
            cols = pl.ds(pl.multiple_of(start + i * COLS, COLS), COLS)
            signal = k_v[here, cols].astype(F32) * v_v[here, cols].astype(F32)
            turned = conv[i * COLS:(i + 1) * COLS, :].T
            g_own[a, :, cols] = (
                q_v[here, cols].astype(F32) * (turned + gain_v[:, cols] * signal)
            ).astype(BF16)

    a2a_arrived(3)
    swaps = []
    backs = []
    parts = []
    step = LANE // PIECES

    def gate_run(a):
        a2a_arrived(4 + a)
        tile = [recv_c[g, :, a * 2 * PART:(a + 1) * 2 * PART, :].astype(F32) for g in range(SETS)]
        other = jnp.concatenate([t[:, PART:] for t in tile], 1).reshape(side, LANE)
        give_c[a] = other.astype(BF16)
        back = swap_cores(2 + a, give_c.at[a], take_c.at[a])
        back.start()
        backs.append(back)
        own = jnp.concatenate([t[:, :PART] for t in tile], 1).reshape(side, LANE)
        gated(a, own, mine)
        back.wait_recv()
        gated(a, take_c[a].astype(F32), theirs)
        for b in range(PIECES):
            i = a * PIECES + b
            here = pl.ds(b * step, step)
            swap = remote(
                g_own.at[a, here], g_near.at[a, here], g_send.at[i], g_recv.at[i], (c, near)
            )
            swap.start()
            swaps.append(swap)

    def product(i, a, here, piece):
        cols = pl.ds(pl.multiple_of(piece * COLS, COLS), COLS)
        return cols, dot(g_own[a, here], w_own[i, :, cols]) + dot(g_near[a, here], w_near[i, :, cols])

    def project_run(a):
        for b in range(PIECES):
            i = a * PIECES + b
            here = slice(b * step, (b + 1) * step)
            swaps[i].wait_recv()

            def project(piece, _):
                cols, sums = product(1, a, here, piece)
                part_out[a, here, cols] = sums.astype(BF16)
                return 0

            lax.fori_loop(0, width // COLS, project, 0)
            rows = pl.ds(b * step, step)
            part = remote(
                part_out.at[a, rows], part_in.at[a, rows], p_send.at[i], p_recv.at[i], (c, far)
            )
            part.start()
            parts.append(part)

    for a in range(runs):
        gate_run(a)
        if a == runs - 1:
            spread(0)
        if a == 0:
            to_sibling(1).wait_recv()
        else:
            project_run(a - 1)
    project_run(runs - 1)
    spread_all(0).wait_recv()
    to_sibling(0).start()
    to_sibling(0).wait_recv()
    for a in range(runs):

        def project_own(piece, _, a=a):
            cols, sums = product(0, a, slice(None), piece)
            part_own[a, :, cols] = sums
            return 0

        lax.fori_loop(0, width // COLS, project_own, 0)
    stores = []
    for a in range(runs):
        for b in range(PIECES):
            i = a * PIECES + b
            here = slice(b * step, (b + 1) * step)
            parts[i].wait_recv()
            out_v[a, here] = (part_own[a, here] + part_in[a, here].astype(F32)).astype(BF16)
            store = pltpu.make_async_copy(
                out_v.at[a, pl.ds(b * step, step)],
                out_hbm.at[pl.ds(a * LANE + b * step, step)],
                store_sem.at[i],
            )
            store.start()
            stores.append(store)

    for store in stores:
        store.wait()
    for i in range(len(moves)):
        a2a_all(i).wait_send()
    for i in range(2):
        spread_all(i).wait_send()
        to_sibling(i).wait_send()
    for copy in near_copies + [swap_f, swap_s] + backs + swaps + parts:
        copy.wait_send()


def per_device(query_proj, key_proj, value_proj, filter_taps, skip_gain, out_weight):
    chips = lax.axis_size("ctx") // 2
    rows, width = query_proj.shape
    runs = rows // LANE
    side = width // 2
    half = chips * runs * 2
    tables = [jnp.asarray(t) for t in dft_tables(chips, runs)]
    gain = skip_gain[None, :]
    dma = pltpu.SemaphoreType.DMA

    def like(x):
        return pltpu.VMEM(x.shape, x.dtype)

    tall = runs * 2 * PART
    flat = pltpu.VMEM((SETS, chips, tall, LANE), BF16)
    swapped = pltpu.VMEM((runs, side, LANE), BF16)
    wide = pltpu.VMEM((chips * tall, LANE), F32)
    weights = pltpu.VMEM((2, width, width), BF16)
    piece = pltpu.VMEM((runs, LANE, width), BF16)
    moves = 1 + SETS + 1 + runs
    return pl.pallas_call(
        functools.partial(whole_kernel, chips, runs, width),
        out_shape=jax.ShapeDtypeStruct((rows, width), BF16),
        in_specs=[pl.BlockSpec(memory_space=pl.ANY)] * (6 + len(tables)),
        out_specs=pl.BlockSpec(memory_space=pl.ANY),
        scratch_shapes=[
            like(query_proj), like(key_proj), like(value_proj), like(filter_taps), like(gain),
            weights, weights,
            *[like(t) for t in tables],
            *[swapped] * 8,
            *[flat] * 6,
            wide, wide, pltpu.VMEM((SETS * PART, half, 2 * LANE), F32),
            piece, piece, piece, piece, pltpu.VMEM((runs, LANE, width), F32), piece,
            dma((7,)), dma((len(tables),)), dma((moves,)), dma((runs * PIECES,)),
            dma((moves,)), dma((moves,)), dma((2 + runs,)), dma((2 + runs,)),
            dma((2,)), dma((2,)), dma((2,)), dma((2,)), dma((2,)), dma((2,)),
            *[dma((runs * PIECES,))] * 4,
        ],
        compiler_params=pltpu.CompilerParams(
            collective_id=0, has_side_effects=True, vmem_limit_bytes=56 * 1024 * 1024
        ),
    )(query_proj, key_proj, value_proj, filter_taps, gain, out_weight, *tables)


def solution(mesh):
    placed = (
        P("ctx", "chan"),
        P("ctx", "chan"),
        P("ctx", "chan"),
        P("ctx", "chan"),
        P("chan"),
        P("chan", None),
    )
    return jax.shard_map(
        per_device, mesh=mesh, in_specs=placed, out_specs=P("ctx", "chan"), check_vma=False
    )
```
